32 devices in a mesh: groups: 2 (over y), rows: 4 (over z), sub: 2 (over x), cols: 2 (over core).
Axes of the slice: x: 2, y: 2, z: 4, core: 2. Of those that a mesh axis runs over, the one named last changes fastest.
Arguments:
- noise: bfloat16 [16384, 256], P(('groups', 'rows', 'sub'), 'cols'), parts along dimension 0, may hold values from -6 to 6
- bases: bfloat16 [2, 16384, 256], P(None, ('groups', 'rows', 'sub')), parts along dimension 1, may hold values from -0.375 to 0.375
- cores: bfloat16 [6, 256, 256], P('groups'), parts along dimension 0, may hold values from -0.09375 to 0.09375
- self_mob: float32 [16384], P(('groups', 'rows', 'sub')), parts along dimension 0, may hold values from 0.5 to 2
Outputs:
- displace: float32 [16384, 256], P(('groups', 'rows', 'sub'), 'cols'), parts along dimension 0
The draws below stay inside these ranges and needn't reach their ends.
There are 2 independent parts, one for each index of `groups`. The reference program is written for one: setup_inputs(seed, part) draws one part's arguments, and reference() takes and returns one part's arrays. A program takes and returns all parts, laid end to end along the dimension named above; each array names one. Nothing has to cross between parts.
All inputs are finite; a program needn't handle non-finite values.
Results may differ from the reference program's by a relative error of at most 0.0022.
Values may be sent and summed in bfloat16 or wider, within the bound.
A program may use at most 64 MiB of HBM per device.

```python
import math
import jax
import jax.numpy as jnp
from jax import lax

K = 256
COLS = 256
LEVELS = 2
PAIRS = 3
BEADS = 8192


def block_levels(own_key, shape, split, low, high):
    level, own = 1.0, jax.random.fold_in(own_key, 6)
    for dim, parts in split:
        heights = jnp.exp(jax.random.uniform(jax.random.fold_in(own, dim), (parts,), jnp.float32, low / len(split), high / len(split)))
        level = level * jnp.repeat(heights, shape[dim] // parts).reshape([-1 if axis == dim else 1 for axis in range(len(shape))])
    return level


def gaussian(key, extent, scale, most, split=(), kind=jnp.bfloat16):
    array = jax.random.normal(key, extent, jnp.float32) * scale
    if len(split) > 0:
        array = block_levels(key, extent, split, -0.22, 0.18) * array
    return jnp.clip(array, min=-most, max=most).astype(kind)


def setup_inputs(seed: int = 0, part: int = 0) -> dict:
    key_list = jax.random.split(jax.random.key(seed), 5)
    part_keys = jax.random.split(jax.random.fold_in(key_list[4], part), 5)
    return {
        "noise": gaussian(part_keys[0], (BEADS, COLS), 1.0, 6.0, ((0, 8), (1, 2))),
        "bases": gaussian(part_keys[1], (LEVELS, BEADS, K), K ** -0.5, 0.375, ((1, 8),)),
        "cores": gaussian(part_keys[2], (PAIRS, K, K), (BEADS // 2) ** -0.5, 0.09375),
        "self_mob": jnp.clip(jnp.exp(math.log(2.0) - 1.3862944 * jax.random.uniform(part_keys[3], (BEADS,), jnp.float32) ** block_levels(part_keys[3], (BEADS,), ((0, 8),), -0.2, 0.2)), 0.5, 2.0),
    }


def reference(noise, bases, cores, self_mob):
    total = noise.shape[0]
    rank = bases.shape[2]
    width = noise.shape[1]
    result = self_mob[:, None] * noise.astype(jnp.float32)
    for level in range(1, LEVELS + 1):
        nodes = 2 ** level
        size = total // nodes
        basis = bases[level - 1].reshape(nodes, size, rank).astype(jnp.float32)
        signal = noise.reshape(nodes, size, width).astype(jnp.float32)
        proj = jnp.einsum('nsk,nsc->nkc', basis, signal, precision=lax.Precision.HIGHEST)
        other = proj.reshape(nodes // 2, 2, rank, width)[:, ::-1].reshape(nodes, rank, width)
        chosen = cores[2 ** (level - 1) - 1:2 ** level - 1].astype(jnp.float32)
        paired = jnp.stack([chosen, jnp.transpose(chosen, (0, 2, 1))], axis=1).reshape(nodes, rank, rank)
        mapped = jnp.einsum('nij,njc->nic', paired, other, precision=lax.Precision.HIGHEST)
        mapped = mapped.astype(jnp.bfloat16).astype(jnp.float32)
        added = jnp.einsum('nsk,nkc->nsc', basis, mapped, precision=lax.Precision.HIGHEST)
        result = result + added.reshape(total, width)
    return result
```

```python
import functools

import jax
import jax.numpy as jnp
from jax import lax
from jax.experimental import pallas as pl
from jax.experimental.pallas import tpu as pltpu
from jax.sharding import PartitionSpec as P

MIN_SLICE = 16
MESH = pl.DeviceIdType.MESH
NT = (((1,), (1,)), ((), ()))
NN = (((1,), (0,)), ((), ()))


def flip(index, mask):
    bit = 1
    while bit <= mask:
        if mask & bit:
            index = index + bit * (1 - 2 * (lax.div(index, bit) % 2))
        bit *= 2
    return index


def plan(rows, sub, width, levels):
    out = []
    for level in range(1, levels + 1):
        group = rows // 2 ** (level - 1) * sub
        reducers = min(group, width // MIN_SLICE)
        out.append((group, reducers, width // reducers))
    return out


def halves(value):
    first = value.astype(jnp.bfloat16)
    rest = value - first.astype(jnp.float32)
    second = rest.astype(jnp.bfloat16)
    third = (rest - second.astype(jnp.float32)).astype(jnp.bfloat16)
    return jnp.concatenate([first, second, third], axis=0)


def kernel(rows, sub, levels, block, refs_per_level, *refs):
    noise_hbm, bases_hbm, cores_hbm, mob_ref, out_hbm = refs[:5]
    noise_v, bases_v, cores_v, turned, total, in_sem, base_sem, core_sem, out_sem = refs[5:14]
    per_level = [
        refs[14 + refs_per_level * l : 14 + refs_per_level * (l + 1)] for l in range(levels)
    ]
    beads, width = noise_v.shape
    row, half = lax.axis_index("rows"), lax.axis_index("sub")
    place = row * sub + half
    sizes = plan(rows, sub, width, levels)

    def device(position):
        return {"rows": lax.div(position, sub), "sub": position % sub}

    load_noise = pltpu.make_async_copy(noise_hbm, noise_v, in_sem)
    load_noise.start()
    loads = []
    for l in range(levels):
        loads.append(pltpu.make_async_copy(bases_hbm.at[l], bases_v.at[l], base_sem.at[l]))
        loads[-1].start()
    core_loads = []
    for l in range(levels):
        pair = 2**l - 1 + lax.div(row, rows // 2**l)
        core_loads.append(
            pltpu.make_async_copy(cores_hbm.at[pair], cores_v.at[l], core_sem.at[l])
        )
        core_loads[-1].start()

    barrier = pltpu.get_barrier_semaphore()
    everyone = rows * sub
    for mask in range(1, everyone):
        pl.semaphore_signal(
            barrier, inc=1, device_id=device(flip(place, mask)), device_id_type=MESH
        )

    load_noise.wait()
    for start in range(0, beads, block):
        turned[:, start : start + block] = noise_v[start : start + block, :].T

    sent = []
    for l in range(levels):
        group, reducers, cut = sizes[l]
        proj, got, _, _, send_sem, got_sem, _, _ = per_level[l]
        loads[l].wait()
        part = None
        for start in range(0, beads, block):
            term = lax.dot_general(
                turned[:, start : start + block],
                bases_v[l, start : start + block, :],
                NN,
                preferred_element_type=jnp.float32,
            )
            part = term if part is None else part + term
        proj[...] = part
        if l == 0:
            pl.semaphore_wait(barrier, everyone - 1)
        inner = place % group
        start_of_group = place - inner
        low = inner % reducers
        high = lax.div(inner, reducers)
        copies = []
        for mask in reversed(range(reducers)):
            target = flip(low, mask)
            copy = pltpu.make_async_remote_copy(
                src_ref=proj.at[pl.ds(pl.multiple_of(target * cut, cut), cut)],
                dst_ref=got.at[high * reducers + mask if group > reducers else mask],
                send_sem=send_sem.at[mask],
                recv_sem=got_sem.at[high * reducers + mask if group > reducers else mask],
                device_id=device(start_of_group + target),
                device_id_type=MESH,
            )
            if mask > 0:
                copy.start()
            elif group > reducers:
                pl.when(high > 0)(copy.start)
            copies.append((mask, copy))
        sent.append(copies)

    mob = mob_ref[...].T
    for i in range(beads // 128):
        piece = slice(i * 128, (i + 1) * 128)
        total[piece, :] = mob[:, i : i + 1] * noise_v[piece, :].astype(jnp.float32)

    pending = []
    for l in range(levels):
        group, reducers, cut = sizes[l]
        proj, got, staged, mapped, _, got_sem, z_send, z_sem = per_level[l]
        inner = place % group
        start_of_group = place - inner
        low = inner % reducers
        high = lax.div(inner, reducers)
        own_rows = pl.ds(pl.multiple_of(low * cut, cut), cut)
        even = inner < group // 2
        core_loads[l].wait()

        def reduce(l=l, group=group, reducers=reducers, cut=cut, proj=proj, got=got,
                   staged=staged, mapped=mapped, got_sem=got_sem, z_send=z_send, z_sem=z_sem,
                   inner=inner, start_of_group=start_of_group, low=low, own_rows=own_rows, even=even):
            for slot in range(1, group):
                pltpu.make_async_copy(got.at[slot], got.at[slot], got_sem.at[slot]).wait()
            same = proj[own_rows, :]
            for slot in range(1, group // 2):
                same = same + got[slot]
            other = got[group // 2]
            for slot in range(group // 2 + 1, group):
                other = other + got[slot]
            core = cores_v[l]
            on_even = jnp.where(even, same, other)
            on_odd = jnp.where(even, other, same)
            for_even = lax.dot_general(halves(on_odd), core, NT, preferred_element_type=jnp.float32)
            for_odd = lax.dot_general(halves(on_even), core, NN, preferred_element_type=jnp.float32)
            for_even = for_even[2 * cut :] + for_even[cut : 2 * cut] + for_even[:cut]
            for_odd = for_odd[2 * cut :] + for_odd[cut : 2 * cut] + for_odd[:cut]
            mine = jnp.where(even, for_even, for_odd).astype(jnp.bfloat16)
            theirs = jnp.where(even, for_odd, for_even).astype(jnp.bfloat16)
            staged[0] = mine
            staged[1] = theirs
            mapped[own_rows, :] = mine
            copies = []
            for mask in reversed(range(1, group)):
                copy = pltpu.make_async_remote_copy(
                    src_ref=staged.at[0 if mask < group // 2 else 1],
                    dst_ref=mapped.at[own_rows],
                    send_sem=z_send.at[mask],
                    recv_sem=z_sem.at[mask % reducers],
                    device_id=device(start_of_group + flip(inner, mask)),
                    device_id_type=MESH,
                )
                copy.start()
                copies.append(copy)
            if group > reducers:
                for copy in copies:
                    copy.wait_send()
            return copies

        if group > reducers:
            @pl.when(high == 0)
            def _(reduce=reduce):
                reduce()
        else:
            pending += reduce()

    for l in reversed(range(levels)):
        group, reducers, cut = sizes[l]
        _, _, _, mapped, send_sem, _, _, z_sem = per_level[l]
        inner = place % group
        low = inner % reducers
        high = lax.div(inner, reducers)
        for mask in range(reducers):
            source = flip(low, mask)
            piece = mapped.at[pl.ds(pl.multiple_of(source * cut, cut), cut)]
            arrived = pltpu.make_async_copy(piece, piece, z_sem.at[mask])
            if mask > 0:
                arrived.wait()
            elif group > reducers:
                pl.when(high > 0)(arrived.wait)
        for start in range(0, beads, block):
            piece = slice(start, start + block)
            total[piece, :] += lax.dot_general(
                bases_v[l, piece, :], mapped[...], NT, preferred_element_type=jnp.float32
            )
            if l == 0:
                pltpu.make_async_copy(
                    total.at[piece], out_hbm.at[piece], out_sem.at[start // block]
                ).start()
    for l in range(levels):
        group, reducers, _ = sizes[l]
        high = lax.div(place % group, reducers)
        for mask, copy in sent[l]:
            if mask > 0:
                copy.wait_send()
            elif group > reducers:
                pl.when(high > 0)(copy.wait_send)
    for copy in pending:
        copy.wait_send()
    for start in range(0, beads, block):
        piece = slice(start, start + block)
        pltpu.make_async_copy(
            total.at[piece], out_hbm.at[piece], out_sem.at[start // block]
        ).wait()


def per_device(noise, bases, cores, self_mob):
    rows, sub = lax.axis_size("rows"), lax.axis_size("sub")
    levels, beads, rank = bases.shape
    width = noise.shape[1]
    block = min(beads, 512)
    scratch = [
        pltpu.VMEM((beads, width), noise.dtype),
        pltpu.VMEM(bases.shape, bases.dtype),
        pltpu.VMEM((levels, rank, rank), cores.dtype),
        pltpu.VMEM((width, beads), noise.dtype),
        pltpu.VMEM((beads, width), jnp.float32),
        pltpu.SemaphoreType.DMA(()),
        pltpu.SemaphoreType.DMA((levels,)),
        pltpu.SemaphoreType.DMA((levels,)),
        pltpu.SemaphoreType.DMA((beads // block,)),
    ]
    for group, reducers, cut in plan(rows, sub, width, levels):
        scratch += [
            pltpu.VMEM((width, rank), jnp.float32),
            pltpu.VMEM((group, cut, rank), jnp.float32),
            pltpu.VMEM((2, cut, rank), jnp.bfloat16),
            pltpu.VMEM((width, rank), jnp.bfloat16),
            pltpu.SemaphoreType.DMA((reducers,)),
            pltpu.SemaphoreType.DMA((group,)),
            pltpu.SemaphoreType.DMA((group,)),
            pltpu.SemaphoreType.DMA((reducers,)),
        ]
    return pl.pallas_call(
        functools.partial(kernel, rows, sub, levels, block, 8),
        out_shape=jax.ShapeDtypeStruct((beads, width), jnp.float32),
        in_specs=[pl.BlockSpec(memory_space=pl.ANY)] * 3 + [pl.BlockSpec(memory_space=pltpu.VMEM)],
        out_specs=pl.BlockSpec(memory_space=pl.ANY),
        scratch_shapes=scratch,
        compiler_params=pltpu.CompilerParams(
            collective_id=0, has_side_effects=True, vmem_limit_bytes=40 * 2**20
        ),
    )(noise, bases, cores, self_mob.reshape(beads // 128, 128))


def solution(mesh):
    in_specs = (
        P(("groups", "rows", "sub"), "cols"),
        P(None, ("groups", "rows", "sub"), None),
        P("groups", None, None),
        P(("groups", "rows", "sub")),
    )
    out_specs = P(("groups", "rows", "sub"), "cols")
    return jax.shard_map(
        per_device, mesh=mesh, in_specs=in_specs, out_specs=out_specs, check_vma=False
    )
```

```python
import functools

import jax
import jax.numpy as jnp
from jax import lax
from jax.experimental import pallas as pl
from jax.experimental.pallas import tpu as pltpu
from jax.sharding import PartitionSpec as P

MIN_SLICE = 16
MESH = pl.DeviceIdType.MESH
NT = (((1,), (1,)), ((), ()))
NN = (((1,), (0,)), ((), ()))


def flip(index, mask):
    bit = 1
    while bit <= mask:
        if mask & bit:
            index = index + bit * (1 - 2 * (lax.div(index, bit) % 2))
        bit *= 2
    return index


def plan(rows, sub, width, levels):
    out = []
    for level in range(1, levels + 1):
        group = rows // 2 ** (level - 1) * sub
        reducers = min(group, width // MIN_SLICE)
        out.append((group, reducers, width // reducers))
    return out


def halves(value):
    first = value.astype(jnp.bfloat16)
    rest = value - first.astype(jnp.float32)
    second = rest.astype(jnp.bfloat16)
    third = (rest - second.astype(jnp.float32)).astype(jnp.bfloat16)
    return jnp.concatenate([first, second, third], axis=0)


def kernel(rows, sub, levels, block, refs_per_level, *refs):
    noise_hbm, bases_hbm, cores_hbm, mob_hbm, total = refs[:5]
    noise_v, bases_v, cores_v, turned, mob_v, in_sem, base_sem, core_sem, mob_sem = refs[5:14]
    per_level = [
        refs[14 + refs_per_level * l : 14 + refs_per_level * (l + 1)] for l in range(levels)
    ]
    beads, width = noise_v.shape
    row, half = lax.axis_index("rows"), lax.axis_index("sub")
    place = row * sub + half
    sizes = plan(rows, sub, width, levels)

    def device(position):
        return {"rows": lax.div(position, sub), "sub": position % sub}

    load_noise = pltpu.make_async_copy(noise_hbm, noise_v, in_sem)
    load_noise.start()
    loads = []
    for l in range(levels):
        loads.append(pltpu.make_async_copy(bases_hbm.at[l], bases_v.at[l], base_sem.at[l]))
        loads[-1].start()
    core_loads = []
    for l in range(levels):
        pair = 2**l - 1 + lax.div(row, rows // 2**l)
        core_loads.append(
            pltpu.make_async_copy(cores_hbm.at[pair], cores_v.at[l], core_sem.at[l])
        )
        core_loads[-1].start()

    load_mob = pltpu.make_async_copy(mob_hbm, mob_v, mob_sem)
    load_mob.start()

    barrier = pltpu.get_barrier_semaphore()
    everyone = rows * sub
    for mask in range(1, everyone):
        pl.semaphore_signal(
            barrier, inc=1, device_id=device(flip(place, mask)), device_id_type=MESH
        )

    load_noise.wait()
    for start in range(0, beads, block):
        turned[:, start : start + block] = noise_v[start : start + block, :].T

    sent = []
    for l in range(levels):
        group, reducers, cut = sizes[l]
        proj, got, _, _, send_sem, got_sem, _, _ = per_level[l]
        loads[l].wait()
        part = None
        for start in range(0, beads, block):
            term = lax.dot_general(
                turned[:, start : start + block],
                bases_v[l, start : start + block, :],
                NN,
                preferred_element_type=jnp.float32,
            )
            part = term if part is None else part + term
        proj[...] = part
        if l == 0:
            pl.semaphore_wait(barrier, everyone - 1)
        inner = place % group
        start_of_group = place - inner
        low = inner % reducers
        high = lax.div(inner, reducers)
        copies = []
        for mask in reversed(range(reducers)):
            target = flip(low, mask)
            copy = pltpu.make_async_remote_copy(
                src_ref=proj.at[pl.ds(pl.multiple_of(target * cut, cut), cut)],
                dst_ref=got.at[high * reducers + mask if group > reducers else mask],
                send_sem=send_sem.at[mask],
                recv_sem=got_sem.at[high * reducers + mask if group > reducers else mask],
                device_id=device(start_of_group + target),
                device_id_type=MESH,
            )
            if mask > 0:
                copy.start()
            elif group > reducers:
                pl.when(high > 0)(copy.start)
            copies.append((mask, copy))
        sent.append(copies)

    load_mob.wait()
    mob = mob_v[...].T
    for i in range(beads // 128):
        piece = slice(i * 128, (i + 1) * 128)
        total[piece, :] = mob[:, i : i + 1] * noise_v[piece, :].astype(jnp.float32)

    pending = []
    for l in range(levels):
        group, reducers, cut = sizes[l]
        proj, got, staged, mapped, _, got_sem, z_send, z_sem = per_level[l]
        inner = place % group
        start_of_group = place - inner
        low = inner % reducers
        high = lax.div(inner, reducers)
        own_rows = pl.ds(pl.multiple_of(low * cut, cut), cut)
        even = inner < group // 2
        core_loads[l].wait()

        def reduce(l=l, group=group, reducers=reducers, cut=cut, proj=proj, got=got,
                   staged=staged, mapped=mapped, got_sem=got_sem, z_send=z_send, z_sem=z_sem,
                   inner=inner, start_of_group=start_of_group, low=low, own_rows=own_rows, even=even):
            for slot in range(1, group):
                pltpu.make_async_copy(got.at[slot], got.at[slot], got_sem.at[slot]).wait()
            same = proj[own_rows, :]
            for slot in range(1, group // 2):
                same = same + got[slot]
            other = got[group // 2]
            for slot in range(group // 2 + 1, group):
                other = other + got[slot]
            core = cores_v[l]
            on_even = jnp.where(even, same, other)
            on_odd = jnp.where(even, other, same)
            for_even = lax.dot_general(halves(on_odd), core, NT, preferred_element_type=jnp.float32)
            for_odd = lax.dot_general(halves(on_even), core, NN, preferred_element_type=jnp.float32)
            for_even = for_even[2 * cut :] + for_even[cut : 2 * cut] + for_even[:cut]
            for_odd = for_odd[2 * cut :] + for_odd[cut : 2 * cut] + for_odd[:cut]
            mine = jnp.where(even, for_even, for_odd).astype(jnp.bfloat16)
            theirs = jnp.where(even, for_odd, for_even).astype(jnp.bfloat16)
            staged[0] = mine
            staged[1] = theirs
            mapped[own_rows, :] = mine
            copies = []
            for mask in reversed(range(1, group)):
                copy = pltpu.make_async_remote_copy(
                    src_ref=staged.at[0 if mask < group // 2 else 1],
                    dst_ref=mapped.at[own_rows],
                    send_sem=z_send.at[mask],
                    recv_sem=z_sem.at[mask % reducers],
                    device_id=device(start_of_group + flip(inner, mask)),
                    device_id_type=MESH,
                )
                copy.start()
                copies.append(copy)
            if group > reducers:
                for copy in copies:
                    copy.wait_send()
            return copies

        if group > reducers:
            @pl.when(high == 0)
            def _(reduce=reduce):
                reduce()
        else:
            pending += reduce()

    for l in reversed(range(levels)):
        group, reducers, cut = sizes[l]
        _, _, _, mapped, send_sem, _, _, z_sem = per_level[l]
        inner = place % group
        low = inner % reducers
        high = lax.div(inner, reducers)
        for mask in range(reducers):
            source = flip(low, mask)
            piece = mapped.at[pl.ds(pl.multiple_of(source * cut, cut), cut)]
            arrived = pltpu.make_async_copy(piece, piece, z_sem.at[mask])
            if mask > 0:
                arrived.wait()
            elif group > reducers:
                pl.when(high > 0)(arrived.wait)
        for start in range(0, beads, block):
            piece = slice(start, start + block)
            total[piece, :] += lax.dot_general(
                bases_v[l, piece, :], mapped[...], NT, preferred_element_type=jnp.float32
            )
    for l in range(levels):
        group, reducers, _ = sizes[l]
        high = lax.div(place % group, reducers)
        for mask, copy in sent[l]:
            if mask > 0:
                copy.wait_send()
            elif group > reducers:
                pl.when(high > 0)(copy.wait_send)
    for copy in pending:
        copy.wait_send()


def per_device(noise, bases, cores, self_mob):
    rows, sub = lax.axis_size("rows"), lax.axis_size("sub")
    levels, beads, rank = bases.shape
    width = noise.shape[1]
    block = min(beads, 512)
    scratch = [
        pltpu.VMEM((beads, width), noise.dtype),
        pltpu.VMEM(bases.shape, bases.dtype),
        pltpu.VMEM((levels, rank, rank), cores.dtype),
        pltpu.VMEM((width, beads), noise.dtype),
        pltpu.VMEM((beads // 128, 128), jnp.float32),
        pltpu.SemaphoreType.DMA(()),
        pltpu.SemaphoreType.DMA((levels,)),
        pltpu.SemaphoreType.DMA((levels,)),
        pltpu.SemaphoreType.DMA(()),
    ]
    for group, reducers, cut in plan(rows, sub, width, levels):
        scratch += [
            pltpu.VMEM((width, rank), jnp.float32),
            pltpu.VMEM((group, cut, rank), jnp.float32),
            pltpu.VMEM((2, cut, rank), jnp.bfloat16),
            pltpu.VMEM((width, rank), jnp.bfloat16),
            pltpu.SemaphoreType.DMA((reducers,)),
            pltpu.SemaphoreType.DMA((group,)),
            pltpu.SemaphoreType.DMA((group,)),
            pltpu.SemaphoreType.DMA((reducers,)),
        ]
    return pl.pallas_call(
        functools.partial(kernel, rows, sub, levels, block, 8),
        out_shape=jax.ShapeDtypeStruct((beads, width), jnp.float32),
        in_specs=[pl.BlockSpec(memory_space=pltpu.HBM)] * 4,
        out_specs=pl.BlockSpec(memory_space=pltpu.VMEM),
        scratch_shapes=scratch,
        compiler_params=pltpu.CompilerParams(
            collective_id=0, has_side_effects=True, vmem_limit_bytes=40 * 2**20
        ),
    )(*[pltpu.with_memory_space_constraint(x, pltpu.HBM) for x in (noise, bases, cores, self_mob.reshape(beads // 128, 128))])


def solution(mesh):
    in_specs = (
        P(("groups", "rows", "sub"), "cols"),
        P(None, ("groups", "rows", "sub"), None),
        P("groups", None, None),
        P(("groups", "rows", "sub")),
    )
    out_specs = P(("groups", "rows", "sub"), "cols")
    return jax.shard_map(
        per_device, mesh=mesh, in_specs=in_specs, out_specs=out_specs, check_vma=False
    )
```

```python
import functools

import jax
import jax.numpy as jnp
from jax import lax
from jax.experimental import pallas as pl
from jax.experimental.pallas import tpu as pltpu
from jax.sharding import PartitionSpec as P

MIN_SLICE = 16
MESH = pl.DeviceIdType.MESH
NT = (((1,), (1,)), ((), ()))
NN = (((1,), (0,)), ((), ()))


def flip(index, mask):
    bit = 1
    while bit <= mask:
        if mask & bit:
            index = index + bit * (1 - 2 * (lax.div(index, bit) % 2))
        bit *= 2
    return index


def plan(rows, sub, width, levels):
    out = []
    for level in range(1, levels + 1):
        group = rows // 2 ** (level - 1) * sub
        reducers = min(group, width // MIN_SLICE)
        out.append((group, reducers, width // reducers))
    return out


def halves(value):
    first = value.astype(jnp.bfloat16)
    rest = value - first.astype(jnp.float32)
    second = rest.astype(jnp.bfloat16)
    third = (rest - second.astype(jnp.float32)).astype(jnp.bfloat16)
    return jnp.concatenate([first, second, third], axis=0)


def kernel(rows, sub, cols, levels, block, refs_per_level, *refs):
    noise_hbm, bases_hbm, cores_hbm, mob_hbm, total = refs[:5]
    noise_v, bases_v, cores_v, turned, mob_v, in_sem, base_sem, core_sem, mob_sem = refs[5:14]
    per_level = [
        refs[14 + refs_per_level * l : 14 + refs_per_level * (l + 1)] for l in range(levels)
    ]
    beads, width = noise_v.shape
    row, half, col = lax.axis_index("rows"), lax.axis_index("sub"), lax.axis_index("cols")
    place = row * sub + half
    last = cols - 1
    on_last = col == last
    sizes = plan(rows, sub, width, levels)

    def device(position, column):
        return {"rows": lax.div(position, sub), "sub": position % sub, "cols": column}

    load_noise = pltpu.make_async_copy(noise_hbm, noise_v, in_sem)
    load_noise.start()
    loads = []
    for l in range(levels):
        loads.append(pltpu.make_async_copy(bases_hbm.at[l], bases_v.at[l], base_sem.at[l]))
        loads[-1].start()

    barrier = pltpu.get_barrier_semaphore()
    chips = rows * sub

    def greet(position, column):
        pl.semaphore_signal(
            barrier, inc=1, device_id=device(position, column), device_id_type=MESH
        )

    @pl.when(on_last)
    def _():
        for mask in range(chips):
            for column in range(last):
                greet(flip(place, mask), column)

    for mask in range(1, chips):
        greet(flip(place, mask), last)
    pl.when(col < last)(lambda: greet(place, last))

    core_loads = []
    for l in range(levels):
        pair = 2**l - 1 + lax.div(row, rows // 2**l)
        core_loads.append(
            pltpu.make_async_copy(cores_hbm.at[pair], cores_v.at[l], core_sem.at[l])
        )
        core_loads[-1].start()
    load_mob = pltpu.make_async_copy(mob_hbm, mob_v, mob_sem)
    load_mob.start()

    load_noise.wait()
    for start in range(0, beads, block):
        turned[:, start : start + block] = noise_v[start : start + block, :].T

    def spot(l):
        group, reducers, cut = sizes[l]
        inner = place % group
        low = inner % reducers
        high = lax.div(inner, reducers)
        own_rows = pl.ds(pl.multiple_of(low * cut, cut), cut)
        return inner, place - inner, low, high, own_rows

    def is_reducer(l):
        group, reducers, _ = sizes[l]
        if group == reducers:
            return on_last
        return jnp.logical_and(on_last, spot(l)[3] == 0)

    def not_reducer(l):
        group, reducers, _ = sizes[l]
        if group == reducers:
            return col < last
        return jnp.logical_or(col < last, spot(l)[3] > 0)

    def partial_copy(l, mask):
        group, reducers, cut = sizes[l]
        proj, got, _, _, send_sem, got_sem, _, _ = per_level[l]
        _, first, low, high, _ = spot(l)
        target = flip(low, mask)
        slot = col * group + high * reducers + mask
        return pltpu.make_async_remote_copy(
            src_ref=proj.at[pl.ds(pl.multiple_of(target * cut, cut), cut)],
            dst_ref=got.at[slot],
            send_sem=send_sem.at[mask],
            recv_sem=got_sem.at[slot],
            device_id=device(first + target, last),
            device_id_type=MESH,
        )

    def mapped_copies(l):
        group, reducers, _ = sizes[l]
        _, _, staged, mapped, _, _, z_send, z_sem = per_level[l]
        inner, first, _, _, own_rows = spot(l)
        return [
            pltpu.make_async_remote_copy(
                src_ref=staged.at[column * 2 + (0 if mask < group // 2 else 1)],
                dst_ref=mapped.at[own_rows],
                send_sem=z_send.at[column * group + mask],
                recv_sem=z_sem.at[mask % reducers],
                device_id=device(first + flip(inner, mask), column),
                device_id_type=MESH,
            )
            for column in range(cols)
            for mask in reversed(range(group))
            if mask > 0 or column < last
        ]

    for l in range(levels):
        reducers = sizes[l][1]
        proj = per_level[l][0]
        loads[l].wait()
        part = None
        for start in range(0, beads, block):
            term = lax.dot_general(
                turned[:, start : start + block],
                bases_v[l, start : start + block, :],
                NN,
                preferred_element_type=jnp.float32,
            )
            part = term if part is None else part + term
        proj[...] = part
        if l == 0:

            @pl.when(on_last)
            def _():
                pl.semaphore_wait(barrier, chips * cols - 1)

            @pl.when(col < last)
            def _():
                pl.semaphore_wait(barrier, chips)

        for mask in reversed(range(1, reducers)):
            partial_copy(l, mask).start()
        pl.when(not_reducer(l))(lambda l=l: partial_copy(l, 0).start())

    load_mob.wait()
    mob = mob_v[...].T
    for i in range(beads // 128):
        piece = slice(i * 128, (i + 1) * 128)
        total[piece, :] = mob[:, i : i + 1] * noise_v[piece, :].astype(jnp.float32)

    for l in range(levels):
        core_loads[l].wait()

        @pl.when(is_reducer(l))
        def _(l=l):
            group, reducers, cut = sizes[l]
            proj, got, staged, mapped, _, got_sem, _, _ = per_level[l]
            inner, _, _, _, own_rows = spot(l)
            even = inner < group // 2
            for slot in range(cols * group):
                if slot != last * group:
                    pltpu.make_async_copy(got.at[slot], got.at[slot], got_sem.at[slot]).wait()
            on_even, on_odd = [], []
            for column in range(cols):
                base = column * group
                same = proj[own_rows, :] if column == last else got[base]
                for slot in range(1, group // 2):
                    same = same + got[base + slot]
                other = got[base + group // 2]
                for slot in range(group // 2 + 1, group):
                    other = other + got[base + slot]
                on_even.append(jnp.where(even, same, other))
                on_odd.append(jnp.where(even, other, same))
            tall = cols * cut

            def times(value, dims):
                terms = lax.dot_general(
                    halves(jnp.concatenate(value, axis=0)),
                    cores_v[l],
                    dims,
                    preferred_element_type=jnp.float32,
                )
                return terms[2 * tall :] + terms[tall : 2 * tall] + terms[:tall]

            for_even, for_odd = times(on_odd, NT), times(on_even, NN)
            mine = jnp.where(even, for_even, for_odd).astype(jnp.bfloat16)
            theirs = jnp.where(even, for_odd, for_even).astype(jnp.bfloat16)
            for column in range(cols):
                staged[column * 2] = mine[column * cut : (column + 1) * cut]
                staged[column * 2 + 1] = theirs[column * cut : (column + 1) * cut]
            for copy in mapped_copies(l):
                copy.start()
            mapped[own_rows, :] = mine[last * cut :]

    for l in reversed(range(levels)):
        group, reducers, cut = sizes[l]
        mapped, z_sem = per_level[l][3], per_level[l][7]
        low = spot(l)[2]
        for mask in range(reducers):
            source = flip(low, mask)
            piece = mapped.at[pl.ds(pl.multiple_of(source * cut, cut), cut)]
            arrived = pltpu.make_async_copy(piece, piece, z_sem.at[mask])
            if mask > 0:
                arrived.wait()
            else:
                pl.when(not_reducer(l))(arrived.wait)
        for start in range(0, beads, block):
            piece = slice(start, start + block)
            total[piece, :] += lax.dot_general(
                bases_v[l, piece, :], mapped[...], NT, preferred_element_type=jnp.float32
            )
    for l in range(levels):
        for mask in range(1, sizes[l][1]):
            partial_copy(l, mask).wait_send()
        pl.when(not_reducer(l))(lambda l=l: partial_copy(l, 0).wait_send())

        @pl.when(is_reducer(l))
        def _(l=l):
            for copy in mapped_copies(l):
                copy.wait_send()


def per_device(noise, bases, cores, self_mob):
    rows, sub, cols = (lax.axis_size(name) for name in ("rows", "sub", "cols"))
    levels, beads, rank = bases.shape
    width = noise.shape[1]
    block = min(beads, 512)
    scratch = [
        pltpu.VMEM((beads, width), noise.dtype),
        pltpu.VMEM(bases.shape, bases.dtype),
        pltpu.VMEM((levels, rank, rank), cores.dtype),
        pltpu.VMEM((width, beads), noise.dtype),
        pltpu.VMEM((beads // 128, 128), jnp.float32),
        pltpu.SemaphoreType.DMA(()),
        pltpu.SemaphoreType.DMA((levels,)),
        pltpu.SemaphoreType.DMA((levels,)),
        pltpu.SemaphoreType.DMA(()),
    ]
    for group, reducers, cut in plan(rows, sub, width, levels):
        scratch += [
            pltpu.VMEM((width, rank), jnp.float32),
            pltpu.VMEM((cols * group, cut, rank), jnp.float32),
            pltpu.VMEM((2 * cols, cut, rank), jnp.bfloat16),
            pltpu.VMEM((width, rank), jnp.bfloat16),
            pltpu.SemaphoreType.DMA((reducers,)),
            pltpu.SemaphoreType.DMA((cols * group,)),
            pltpu.SemaphoreType.DMA((cols * group,)),
            pltpu.SemaphoreType.DMA((reducers,)),
        ]
    return pl.pallas_call(
        functools.partial(kernel, rows, sub, cols, levels, block, 8),
        out_shape=jax.ShapeDtypeStruct((beads, width), jnp.float32),
        in_specs=[pl.BlockSpec(memory_space=pltpu.HBM)] * 4,
        out_specs=pl.BlockSpec(memory_space=pltpu.VMEM),
        scratch_shapes=scratch,
        compiler_params=pltpu.CompilerParams(
            collective_id=0, has_side_effects=True, vmem_limit_bytes=40 * 2**20
        ),
    )(*[pltpu.with_memory_space_constraint(x, pltpu.HBM) for x in (noise, bases, cores, self_mob.reshape(beads // 128, 128))])


def solution(mesh):
    in_specs = (
        P(("groups", "rows", "sub"), "cols"),
        P(None, ("groups", "rows", "sub"), None),
        P("groups", None, None),
        P(("groups", "rows", "sub")),
    )
    out_specs = P(("groups", "rows", "sub"), "cols")
    return jax.shard_map(
        per_device, mesh=mesh, in_specs=in_specs, out_specs=out_specs, check_vma=False
    )
```
